32 devices in a mesh: freq: 8 (over y, x, core), slab: 4 (over z).
Axes of the slice: x: 2, y: 2, z: 4, core: 2. Of those that a mesh axis runs over, the one named last changes fastest.
Arguments:
- fine_model: bfloat16 [512, 2048], P(('freq', 'slab')), may hold values from 0.5 to 2
- resample: bfloat16 [8, 512, 512], P('freq', 'slab'), may hold values from -0.25 to 0.25
- lateral: bfloat16 [2048, 2048], replicated, may hold values from -0.0625 to 0.0625
- shift: float32 [8], P('freq'), may hold values from 0.5 to 4
- source: float32 [8, 512, 2048], P('freq', 'slab'), may hold values from -6 to 6
- receiver: float32 [8, 512, 2048], P('freq', 'slab'), may hold values from -6 to 6
Outputs:
- image: float32 [512, 2048], P(('freq', 'slab'))
The draws below stay inside these ranges and needn't reach their ends.
All inputs are finite; a program needn't handle non-finite values.
Results may differ from the reference program's by a relative error of at most 0.0029.
Values may be sent and summed in bfloat16 or wider, within the bound.
No kernel may reach another device: no remote copies, remote signals or barrier semaphores. Data moves between devices by JAX's collectives and lax.ppermute only.
A program may use at most 128 MiB of HBM per device.

```python
import math
import jax
import jax.numpy as jnp
from jax import lax

NL = 2048
SWEEPS = 8
NGROUPS = 8
NZF = 512
CZT = 512


def levels(rng, shape, split, smallest, largest):
    loudness, own = 1.0, jax.random.fold_in(rng, 6)
    for axis_at, shards_of in split:
        heights = jnp.exp(jax.random.uniform(jax.random.fold_in(own, axis_at), (shards_of,), jnp.float32, smallest / len(split), largest / len(split)))
        loudness = loudness * jnp.repeat(heights, shape[axis_at] // shards_of).reshape([-1 if axis == axis_at else 1 for axis in range(len(shape))])
    return loudness


def noise(rng, extent, scale, most, cuts=(), dtype=jnp.bfloat16):
    entries = jax.random.normal(rng, extent, jnp.float32) * scale
    if len(cuts) > 0:
        entries = levels(rng, extent, cuts, -0.22, 0.18) * entries
    return jnp.clip(entries, min=-most, max=most).astype(dtype)


def setup_inputs(seed: int = 0) -> dict:
    splits = jax.random.split(jax.random.key(seed), 7)
    fine_model = jnp.clip(0.5 + 1.5 * jax.random.uniform(splits[0], (NZF, NL), jnp.float32) ** levels(splits[0], (NZF, NL), ((0, 32),), -0.2, 0.2), 0.5, 2.0).astype(jnp.bfloat16)
    resample = noise(splits[1], (NGROUPS, CZT, NZF), NZF ** -0.5, 0.25, ((0, 8), (1, 4)))
    lateral = noise(splits[2], (NL, NL), (4 * NL) ** -0.5, 0.0625)
    shift = jnp.clip(jnp.exp(math.log(4.0) - 2.0794415 * jax.random.uniform(splits[3], (NGROUPS,), jnp.float32) ** levels(splits[3], (NGROUPS,), ((0, 8),), -0.2, 0.2)), 0.5, 4.0)
    source = noise(splits[4], (NGROUPS, CZT, NL), 1.0, 6.0, ((0, 8), (1, 4)), jnp.float32)
    receiver = noise(splits[5], (NGROUPS, CZT, NL), 1.0, 6.0, ((0, 8), (1, 4)), jnp.float32)
    return dict(fine_model=fine_model, resample=resample, lateral=lateral, shift=shift, source=source, receiver=receiver)


def reference(fine_model, resample, lateral, shift, source, receiver):
    def group(total, items):
        oper, factor, src, rec = items
        coarse = jnp.dot(oper, fine_model, preferred_element_type=jnp.float32)
        diag = 4.0 + factor * coarse * coarse
        field = jnp.zeros(src.shape, jnp.float32)
        for sweep in range(SWEEPS):
            padded = jnp.pad(field, ((1, 1), (0, 0)))
            beside = padded[2:] + padded[:-2]
            side = jnp.dot(field.astype(jnp.bfloat16), lateral, preferred_element_type=jnp.float32)
            field = (src + 0.5 * beside + side) / diag
        partial_img = (field * rec).astype(jnp.bfloat16)
        term = lax.dot_general(oper, partial_img, (((0,), (0,)), ((), ())), preferred_element_type=jnp.float32)
        return total + term, None

    start = jnp.zeros(fine_model.shape, jnp.float32)
    image, unused = lax.scan(group, start, (resample, shift, source, receiver))
    return image
```

```python
import functools

import jax
import jax.numpy as jnp
from jax import lax
from jax.experimental import pallas as pl
from jax.experimental.pallas import tpu as pltpu
from jax.sharding import PartitionSpec as P

SWEEPS = 8
HALO = 8
TILE = 256
MIB = 1 << 20
VMEM = pl.BlockSpec(memory_space=pltpu.VMEM)
SMEM = pl.BlockSpec(memory_space=pltpu.SMEM)


def xor_permute(value, axis, mask):
    size = lax.axis_size(axis)
    return lax.ppermute(value, axis, [(i, i ^ mask) for i in range(size)])


def solve_kernel(n_freq, n_slab, where, factor, *refs):
    blocks = refs[:n_freq]
    oper, oper_up, oper_down, src, src_up, src_down, rec, lateral, out = refs[n_freq : n_freq + 9]
    fine, rows, source, inverse, field, field_lo = refs[n_freq + 9 :]
    freq, slab = where[0], where[1]
    depth = src.shape[0]
    width = src.shape[1]
    tall = depth + 2 * HALO
    tile = blocks[0].shape[0] // n_slab
    for g in range(n_freq):
        for j in range(n_slab):
            at = ((freq ^ g) * n_slab + (slab ^ j)) * tile
            fine[pl.ds(pl.multiple_of(at, tile), tile), :] = blocks[g][j * tile : (j + 1) * tile, :]
    rows[0:HALO, :] = oper_up[...]
    rows[HALO : HALO + depth, :] = oper[...].astype(jnp.float32)
    rows[HALO + depth : tall, :] = oper_down[...]
    source[0:HALO, :] = src_up[...]
    source[HALO : HALO + depth, :] = src[...]
    source[HALO + depth : tall, :] = src_down[...]
    basis = rows[...].astype(jnp.bfloat16)
    at = lax.broadcasted_iota(jnp.int32, (tall, TILE), 0) - HALO + slab * depth
    inside = jnp.logical_and(at >= 0, at < n_slab * depth)
    for n in range(0, width, TILE):
        cols = slice(n, n + TILE)
        coarse = jnp.dot(basis, fine[:, cols], preferred_element_type=jnp.float32)
        damped = jnp.where(inside, 1.0 / (4.0 + factor[0] * coarse * coarse), 0.0)
        inverse[:, cols] = damped
        first = source[:, cols] * damped
        field[0, :, cols] = first
        field_lo[0, :, cols] = first.astype(jnp.bfloat16)
    for sweep in range(1, SWEEPS):
        old, new = (sweep - 1) % 2, sweep % 2
        for n in range(0, width, TILE):
            cols = slice(n, n + TILE)
            side = jnp.dot(field_lo[old], lateral[:, cols], preferred_element_type=jnp.float32)
            before = field[old, :, cols]
            beside = pltpu.roll(before, 1, 0) + pltpu.roll(before, tall - 1, 0)
            after = (source[:, cols] + 0.5 * beside + side) * inverse[:, cols]
            if sweep < SWEEPS - 1:
                field[new, :, cols] = after
                field_lo[new, :, cols] = after.astype(jnp.bfloat16)
            else:
                mine = after[HALO : HALO + depth, :]
                out[:, cols] = (mine * rec[:, cols]).astype(jnp.bfloat16)


def back_kernel(n_chips, where, oper, oper_other, part, part_other, keep, *sends):
    freq = where[0]
    core, chip = lax.rem(freq, 2), lax.div(freq, 2)
    half = oper.shape[1] // (2 * n_chips)

    def columns(ref):
        picked = []
        for m in range(n_chips):
            at = pl.multiple_of((chip ^ m) * (2 * half), 2 * half)
            pair = ref[:, pl.ds(at, 2 * half)].astype(jnp.float32)
            picked.append(jnp.where(core == 0, pair[:, :half], pair[:, half:]))
        return jnp.concatenate(picked, axis=1).astype(jnp.bfloat16)

    mine, other = columns(oper), columns(oper_other)
    width = part.shape[1]
    for n in range(0, width, TILE):
        cols = slice(n, n + TILE)
        over = (((0,), (0,)), ((), ()))
        total = lax.dot_general(mine, part[:, cols], over, preferred_element_type=jnp.float32)
        total += lax.dot_general(other, part_other[:, cols], over, preferred_element_type=jnp.float32)
        keep[:, cols] = total[:half]
        for m in range(1, n_chips):
            sends[m - 1][:, cols] = total[m * half : (m + 1) * half].astype(jnp.bfloat16)


def plane_kernel(n_chips, n_slab, where, keep, *refs):
    slab = where[1]
    gets, own, sends = refs[: n_chips - 1], refs[n_chips - 1], refs[n_chips:]
    tile = keep.shape[0] // n_slab
    for j in range(n_slab):
        at = pl.ds(pl.multiple_of((slab ^ j) * tile, tile), tile)
        total = keep[at, :]
        for got in gets:
            total += got[at, :].astype(jnp.float32)
        if j == 0:
            own[...] = total
        else:
            sends[j - 1][...] = total.astype(jnp.bfloat16)


def shards(fine_model, resample, lateral, shift, source, receiver):
    n_freq, n_slab = lax.axis_size("freq"), lax.axis_size("slab")
    n_chips = n_freq // 2
    oper, src, rec = resample[0], source[0], receiver[0]
    depth, width = src.shape
    n_fine = oper.shape[1]
    tall = depth + 2 * HALO
    where = jnp.stack([lax.axis_index("freq"), lax.axis_index("slab")]).astype(jnp.int32)
    f32, bf16 = jnp.float32, jnp.bfloat16

    line = [fine_model] + [xor_permute(fine_model, "slab", m) for m in range(1, n_slab)]
    line = jnp.concatenate(line, axis=0)
    oper_other = xor_permute(oper, "freq", 1)

    edges = jnp.concatenate([src[:HALO], oper[:HALO].astype(f32)], axis=1)
    edges_last = jnp.concatenate([src[depth - HALO :], oper[depth - HALO :].astype(f32)], axis=1)
    line, edges, edges_last = lax.optimization_barrier((line, edges, edges_last))
    plane = [line] + [xor_permute(line, "freq", 2 * m) for m in range(1, n_chips)]
    up = [(i, i + 1) for i in range(n_slab - 1)]
    above = lax.ppermute(edges_last, "slab", up)
    below = lax.ppermute(edges, "slab", [(j, i) for i, j in up])
    blocks = []
    for block in plane:
        blocks += [block, xor_permute(block, "freq", 1)]

    part = pl.pallas_call(
        functools.partial(solve_kernel, n_freq, n_slab),
        out_shape=jax.ShapeDtypeStruct((depth, width), bf16),
        in_specs=[SMEM, SMEM] + [VMEM] * (n_freq + 8),
        out_specs=VMEM,
        scratch_shapes=[
            pltpu.VMEM((n_fine, width), bf16),
            pltpu.VMEM((tall, n_fine), f32),
            pltpu.VMEM((tall, width), f32),
            pltpu.VMEM((tall, width), f32),
            pltpu.VMEM((2, tall, width), f32),
            pltpu.VMEM((2, tall, width), bf16),
        ],
        compiler_params=pltpu.CompilerParams(vmem_limit_bytes=48 * MIB),
        name="solve",
    )(
        where, shift, *blocks, oper, above[:, width:], below[:, width:], src, above[:, :width], below[:, :width],
        rec, lateral,
    )

    part_other = xor_permute(part, "freq", 1)
    rows = n_fine // n_freq
    keep, *sends = pl.pallas_call(
        functools.partial(back_kernel, n_chips),
        out_shape=[jax.ShapeDtypeStruct((rows, width), f32)]
        + [jax.ShapeDtypeStruct((rows, width), bf16)] * (n_chips - 1),
        in_specs=[SMEM] + [VMEM] * 4,
        out_specs=[VMEM] * n_chips,
        compiler_params=pltpu.CompilerParams(vmem_limit_bytes=32 * MIB),
        name="back",
    )(where, oper, oper_other, part, part_other)
    gets = [xor_permute(send, "freq", 2 * (m + 1)) for m, send in enumerate(sends)]

    tile = rows // n_slab
    own, *sends = pl.pallas_call(
        functools.partial(plane_kernel, n_chips, n_slab),
        out_shape=[jax.ShapeDtypeStruct((tile, width), f32)]
        + [jax.ShapeDtypeStruct((tile, width), bf16)] * (n_slab - 1),
        in_specs=[SMEM] + [VMEM] * n_chips,
        out_specs=[VMEM] * n_slab,
        compiler_params=pltpu.CompilerParams(vmem_limit_bytes=32 * MIB),
        name="plane",
    )(where, keep, *gets)
    for m, send in enumerate(sends):
        own = own + xor_permute(send, "slab", m + 1).astype(f32)
    return own


def solution(mesh):
    in_specs = (
        P(("freq", "slab"), None),
        P("freq", "slab", None),
        P(),
        P("freq"),
        P("freq", "slab", None),
        P("freq", "slab", None),
    )
    out_specs = P(("freq", "slab"), None)
    return jax.shard_map(shards, mesh=mesh, in_specs=in_specs, out_specs=out_specs, check_vma=False)
```

```python
import functools

import jax
import jax.numpy as jnp
from jax import lax
from jax.experimental import pallas as pl
from jax.experimental.pallas import tpu as pltpu
from jax.sharding import PartitionSpec as P

SWEEPS = 8
HALO = 8
TILE = 256
MIB = 1 << 20
VMEM = pl.BlockSpec(memory_space=pltpu.VMEM)
SMEM = pl.BlockSpec(memory_space=pltpu.SMEM)


def xor_permute(value, axis, mask):
    size = lax.axis_size(axis)
    return lax.ppermute(value, axis, [(i, i ^ mask) for i in range(size)])


def solve_kernel(n_freq, n_slab, where, factor, *refs):
    blocks = refs[:n_freq]
    oper, oper_up, oper_down, src, src_up, src_down, rec, lateral, out = refs[n_freq : n_freq + 9]
    fine, rows, source, inverse, field, field_lo = refs[n_freq + 9 :]
    freq, slab = where[0], where[1]
    depth = src.shape[0]
    width = src.shape[1]
    tall = depth + 2 * HALO
    tile = blocks[0].shape[0] // n_slab
    for g in range(n_freq):
        for j in range(n_slab):
            at = ((freq ^ g) * n_slab + (slab ^ j)) * tile
            fine[pl.ds(pl.multiple_of(at, tile), tile), :] = blocks[g][j * tile : (j + 1) * tile, :]
    rows[0:HALO, :] = oper_up[...]
    rows[HALO : HALO + depth, :] = oper[...].astype(jnp.float32)
    rows[HALO + depth : tall, :] = oper_down[...]
    source[0:HALO, :] = src_up[...]
    source[HALO : HALO + depth, :] = src[...]
    source[HALO + depth : tall, :] = src_down[...]
    basis = rows[...].astype(jnp.bfloat16)
    at = lax.broadcasted_iota(jnp.int32, (tall, TILE), 0) - HALO + slab * depth
    inside = jnp.logical_and(at >= 0, at < n_slab * depth)
    for n in range(0, width, TILE):
        cols = slice(n, n + TILE)
        coarse = jnp.dot(basis, fine[:, cols], preferred_element_type=jnp.float32)
        damped = jnp.where(inside, 1.0 / (4.0 + factor[0] * coarse * coarse), 0.0)
        inverse[:, cols] = damped
        first = source[:, cols] * damped
        field[0, :, cols] = first
        field_lo[0, :, cols] = first.astype(jnp.bfloat16)
    for sweep in range(1, SWEEPS):
        old, new = (sweep - 1) % 2, sweep % 2
        for n in range(0, width, TILE):
            cols = slice(n, n + TILE)
            side = jnp.dot(field_lo[old], lateral[:, cols], preferred_element_type=jnp.float32)
            before = field[old, :, cols]
            beside = pltpu.roll(before, 1, 0) + pltpu.roll(before, tall - 1, 0)
            after = (source[:, cols] + 0.5 * beside + side) * inverse[:, cols]
            if sweep < SWEEPS - 1:
                field[new, :, cols] = after
                field_lo[new, :, cols] = after.astype(jnp.bfloat16)
            else:
                mine = after[HALO : HALO + depth, :]
                out[:, cols] = (mine * rec[:, cols]).astype(jnp.bfloat16)


def stage_kernel(*refs):
    count = (len(refs) - 1) // 2
    copies = [pltpu.make_async_copy(refs[i], refs[count + i], refs[-1].at[i]) for i in range(count)]
    for copy in copies:
        copy.start()
    for copy in copies:
        copy.wait()


def stage(*arrays):
    return pl.pallas_call(
        stage_kernel,
        out_shape=[pltpu.VMEM(a.shape, a.dtype) for a in arrays],
        in_specs=[pl.BlockSpec(memory_space=pl.ANY)] * len(arrays),
        out_specs=[VMEM] * len(arrays),
        scratch_shapes=[pltpu.SemaphoreType.DMA((len(arrays),))],
        compiler_params=pltpu.CompilerParams(vmem_limit_bytes=48 * MIB),
        cost_estimate=pl.CostEstimate(flops=0, transcendentals=0, bytes_accessed=2 * sum(a.size * a.dtype.itemsize for a in arrays)),
        name="stage",
    )(*arrays)


def back_kernel(n_chips, where, oper, oper_other, part, part_other, keep, *sends):
    freq = where[0]
    core, chip = lax.rem(freq, 2), lax.div(freq, 2)
    half = oper.shape[1] // (2 * n_chips)

    def columns(ref):
        picked = []
        for m in range(n_chips):
            at = pl.multiple_of((chip ^ m) * (2 * half), 2 * half)
            pair = ref[:, pl.ds(at, 2 * half)].astype(jnp.float32)
            picked.append(jnp.where(core == 0, pair[:, :half], pair[:, half:]))
        return jnp.concatenate(picked, axis=1).astype(jnp.bfloat16)

    mine, other = columns(oper), columns(oper_other)
    width = part.shape[1]
    for n in range(0, width, TILE):
        cols = slice(n, n + TILE)
        over = (((0,), (0,)), ((), ()))
        total = lax.dot_general(mine, part[:, cols], over, preferred_element_type=jnp.float32)
        total += lax.dot_general(other, part_other[:, cols], over, preferred_element_type=jnp.float32)
        keep[:, cols] = total[:half]
        for m in range(1, n_chips):
            sends[m - 1][:, cols] = total[m * half : (m + 1) * half].astype(jnp.bfloat16)


def plane_kernel(n_chips, n_slab, where, keep, *refs):
    slab = where[1]
    gets, own, sends = refs[: n_chips - 1], refs[n_chips - 1], refs[n_chips:]
    tile = keep.shape[0] // n_slab
    for j in range(n_slab):
        at = pl.ds(pl.multiple_of((slab ^ j) * tile, tile), tile)
        total = keep[at, :]
        for got in gets:
            total += got[at, :].astype(jnp.float32)
        if j == 0:
            own[...] = total
        else:
            sends[j - 1][...] = total.astype(jnp.bfloat16)


def shards(fine_model, resample, lateral, shift, source, receiver):
    n_freq, n_slab = lax.axis_size("freq"), lax.axis_size("slab")
    n_chips = n_freq // 2
    oper, src, rec = resample[0], source[0], receiver[0]
    depth, width = src.shape
    n_fine = oper.shape[1]
    tall = depth + 2 * HALO
    where = jnp.stack([lax.axis_index("freq"), lax.axis_index("slab")]).astype(jnp.int32)
    f32, bf16 = jnp.float32, jnp.bfloat16

    line = [xor_permute(fine_model, "slab", m) for m in range(n_slab - 1, 0, -1)]
    line = jnp.concatenate([fine_model] + line[::-1], axis=0)
    oper_other = xor_permute(oper, "freq", 1)

    edges = jnp.concatenate([src[:HALO], oper[:HALO].astype(f32)], axis=1)
    edges_last = jnp.concatenate([src[depth - HALO :], oper[depth - HALO :].astype(f32)], axis=1)
    plane = [line] + [xor_permute(line, "freq", 2 * m) for m in range(1, n_chips)]
    odd = lax.rem(lax.axis_index("slab"), 2) == 1
    near = lax.ppermute(jnp.where(odd, edges, edges_last), "slab", [(i, i ^ 1) for i in range(n_slab)])
    mid = [(i, i + 1) for i in range(1, n_slab - 1, 2)]
    far = lax.ppermute(jnp.where(odd, edges_last, edges), "slab", mid + [(j, i) for i, j in mid])
    lateral, src, rec, oper = stage(lateral, src, rec, oper)
    near, far, plane[1] = lax.optimization_barrier((near, far, plane[1]))
    above = jnp.where(odd, near, far)
    below = jnp.where(odd, far, near)
    blocks = []
    for block in plane:
        blocks += [block, xor_permute(block, "freq", 1)]

    part = pl.pallas_call(
        functools.partial(solve_kernel, n_freq, n_slab),
        out_shape=jax.ShapeDtypeStruct((depth, width), bf16),
        in_specs=[SMEM, SMEM] + [VMEM] * (n_freq + 8),
        out_specs=VMEM,
        scratch_shapes=[
            pltpu.VMEM((n_fine, width), bf16),
            pltpu.VMEM((tall, n_fine), f32),
            pltpu.VMEM((tall, width), f32),
            pltpu.VMEM((tall, width), f32),
            pltpu.VMEM((2, tall, width), f32),
            pltpu.VMEM((2, tall, width), bf16),
        ],
        compiler_params=pltpu.CompilerParams(vmem_limit_bytes=12 * MIB),
        name="solve",
    )(
        where, shift, *blocks, oper, above[:, width:], below[:, width:], src, above[:, :width], below[:, :width],
        rec, lateral,
    )

    part_other = xor_permute(part, "freq", 1)
    rows = n_fine // n_freq
    keep, *sends = pl.pallas_call(
        functools.partial(back_kernel, n_chips),
        out_shape=[jax.ShapeDtypeStruct((rows, width), f32)]
        + [jax.ShapeDtypeStruct((rows, width), bf16)] * (n_chips - 1),
        in_specs=[SMEM] + [VMEM] * 4,
        out_specs=[VMEM] * n_chips,
        compiler_params=pltpu.CompilerParams(vmem_limit_bytes=10 * MIB),
        name="back",
    )(where, oper, oper_other, part, part_other)
    gets = [xor_permute(sends[m - 1], "freq", 2 * m) for m in range(n_chips - 1, 0, -1)]

    tile = rows // n_slab
    own, *sends = pl.pallas_call(
        functools.partial(plane_kernel, n_chips, n_slab),
        out_shape=[jax.ShapeDtypeStruct((tile, width), f32)]
        + [jax.ShapeDtypeStruct((tile, width), bf16)] * (n_slab - 1),
        in_specs=[SMEM] + [VMEM] * n_chips,
        out_specs=[VMEM] * n_slab,
        compiler_params=pltpu.CompilerParams(vmem_limit_bytes=10 * MIB),
        name="plane",
    )(where, keep, *gets)
    gets = [xor_permute(sends[m - 1], "slab", m) for m in range(n_slab - 1, 0, -1)]
    for got in gets:
        own = own + got.astype(f32)
    return own


def solution(mesh):
    in_specs = (
        P(("freq", "slab"), None),
        P("freq", "slab", None),
        P(),
        P("freq"),
        P("freq", "slab", None),
        P("freq", "slab", None),
    )
    out_specs = P(("freq", "slab"), None)
    return jax.shard_map(shards, mesh=mesh, in_specs=in_specs, out_specs=out_specs, check_vma=False)
```

```python
import functools

import jax
import jax.numpy as jnp
from jax import lax
from jax.experimental import pallas as pl
from jax.experimental.pallas import tpu as pltpu
from jax.sharding import PartitionSpec as P

SWEEPS = 8
HALO = 8
Z_ORDER = (1, 2, 3)
XY_ORDER = (3, 2, 1)
XYB_ORDER = (3, 2, 1)
ZB_ORDER = (1, 2, 3)
XYB2_ORDER = (1, 2, 3)
TILE = 256
MIB = 1 << 20
VMEM = pl.BlockSpec(memory_space=pltpu.VMEM)
SMEM = pl.BlockSpec(memory_space=pltpu.SMEM)


def xor_permute(value, axis, mask):
    size = lax.axis_size(axis)
    return lax.ppermute(value, axis, [(i, i ^ mask) for i in range(size)])


def solve_kernel(n_blocks, n_slab, where, factor, *refs):
    blocks = refs[:n_blocks]
    oper, oper_up, oper_down, src, src_up, src_down, rec, lateral, moved = refs[n_blocks : n_blocks + 9]
    out, inverse, field, field_lo = refs[n_blocks + 9 :]
    slab = where[1]
    depth, width = src.shape
    tall = depth + 2 * HALO

    def source(cols):
        return jnp.concatenate([src_up[:, cols], src[:, cols], src_down[:, cols]], axis=0)

    rows = jnp.concatenate([oper_up[...], oper[...].astype(jnp.float32), oper_down[...]], axis=0)
    basis = jnp.dot(rows.astype(jnp.bfloat16), moved[...], preferred_element_type=jnp.float32).astype(jnp.bfloat16)
    at = lax.broadcasted_iota(jnp.int32, (tall, TILE), 0) - HALO + slab * depth
    inside = jnp.logical_and(at >= 0, at < n_slab * depth)
    for n in range(0, width, TILE):
        cols = slice(n, n + TILE)
        fine = jnp.concatenate([block[:, cols] for block in blocks], axis=0)
        coarse = jnp.dot(basis, fine, preferred_element_type=jnp.float32)
        damped = jnp.where(inside, 1.0 / (4.0 + factor[0] * coarse * coarse), 0.0)
        inverse[:, cols] = damped
        first = source(cols) * damped
        field[0, :, cols] = first
        field_lo[0, :, cols] = first.astype(jnp.bfloat16)
    for sweep in range(1, SWEEPS - 1):
        old, new = (sweep - 1) % 2, sweep % 2
        for n in range(0, width, TILE):
            cols = slice(n, n + TILE)
            side = jnp.dot(field_lo[old], lateral[:, cols], preferred_element_type=jnp.float32)
            before = field[old, :, cols]
            beside = pltpu.roll(before, 1, 0) + pltpu.roll(before, tall - 1, 0)
            after = (source(cols) + 0.5 * beside + side) * inverse[:, cols]
            field[new, :, cols] = after
            field_lo[new, :, cols] = after.astype(jnp.bfloat16)
    old = (SWEEPS - 2) % 2
    mine = slice(HALO, HALO + depth)
    for n in range(0, width, TILE):
        cols = slice(n, n + TILE)
        side = jnp.dot(field_lo[old], lateral[:, cols], preferred_element_type=jnp.float32)
        before = field[old, :, cols]
        beside = pltpu.roll(before, 1, 0) + pltpu.roll(before, tall - 1, 0)
        after = (src[:, cols] + 0.5 * beside[mine] + side[mine]) * inverse[mine, cols]
        out[:, cols] = (after * rec[:, cols]).astype(jnp.bfloat16)


def stage_kernel(order, n_freq, n_slab, tile, where, oper, oper_other, *refs):
    count = (len(refs) - 4) // 2
    moved, turned, sems, upright = refs[-4:]
    copies = [pltpu.make_async_copy(refs[i], refs[count + i], sems.at[i]) for i in range(count)]
    for copy in copies:
        copy.start()
    freq, slab = where[0], where[1]
    size = moved.shape[0]
    place = lax.broadcasted_iota(jnp.int32, (1, size), 1)
    held = jnp.zeros((1, size), jnp.int32)
    for t, (g, j) in enumerate(order):
        begin = ((freq ^ g) * n_slab + (slab ^ j)) * tile
        held = jnp.where(place >= t * tile, begin + place - t * tile, held)
    step = min(size, 128)
    for n in range(0, size, step):
        row = lax.broadcasted_iota(jnp.int32, (step, size), 0) + n
        moved[n : n + step, :] = jnp.where(row == held, 1.0, 0.0).astype(jnp.bfloat16)
    core, chip = lax.rem(freq, 2), lax.div(freq, 2)
    half = n_slab * tile
    depth = oper.shape[0]
    for m in range(n_freq // 2):
        for b, ref in enumerate((oper, oper_other)):
            at = pl.multiple_of((chip ^ m) * (2 * half), 2 * half)
            pair = ref[:, pl.ds(at, 2 * half)].astype(jnp.float32)
            mine = jnp.where(core == 0, pair[:, :half], pair[:, half:])
            upright[m, :, b * depth : (b + 1) * depth] = mine.T
    for m in range(n_freq // 2):
        for j in range(n_slab):
            at = pl.ds(pl.multiple_of((slab ^ j) * tile, tile), tile)
            begin = m * half + j * tile
            turned[begin : begin + tile, :] = upright[m, at, :].astype(jnp.bfloat16)
    for copy in copies:
        copy.wait()


def stage(where, order, n_freq, n_slab, tile, oper, oper_other, *arrays):
    size, depth = oper.shape[1], oper.shape[0]
    results = [pltpu.VMEM(a.shape, a.dtype) for a in arrays]
    results += [pltpu.VMEM((size, size), jnp.bfloat16), pltpu.VMEM((size // 2, 2 * depth), jnp.bfloat16)]
    held = sum(a.size * a.dtype.itemsize for a in arrays) + 2 * size * size + 2 * size * depth
    return pl.pallas_call(
        functools.partial(stage_kernel, order, n_freq, n_slab, tile),
        out_shape=results,
        in_specs=[SMEM, VMEM, VMEM] + [pl.BlockSpec(memory_space=pl.ANY)] * len(arrays),
        out_specs=[VMEM] * len(results),
        scratch_shapes=[
            pltpu.SemaphoreType.DMA((len(arrays),)),
            pltpu.VMEM((n_freq // 2, n_slab * tile, 2 * depth), jnp.float32),
        ],
        compiler_params=pltpu.CompilerParams(vmem_limit_bytes=58 * MIB - held),
        cost_estimate=cost(0, 2 * held),
        name="stage",
    )(where, oper, oper_other, *arrays)


def back_kernel(n_chips, tile, turned, part, part_other, keep, *sends):
    half, width = keep.shape
    far, near = sends[: n_chips - 1], sends[n_chips - 1 :]
    for n in range(0, width, TILE):
        cols = slice(n, n + TILE)
        both = jnp.concatenate([part[:, cols], part_other[:, cols]], axis=0)
        total = jnp.dot(turned[...], both, preferred_element_type=jnp.float32)
        keep[:, cols] = total[:half]
        for m in range(1, n_chips):
            rows = total[m * half : (m + 1) * half].astype(jnp.bfloat16)
            near[m - 1][:, cols] = rows[:tile]
            far[m - 1][:, cols] = rows[tile:]


def plane_kernel(n_chips, tile, keep, *refs):
    gets, sends = refs[: n_chips - 1], refs[n_chips - 1 :]
    for n in range(0, keep.shape[1], TILE):
        cols = slice(n, n + TILE)
        total = keep[tile:, cols]
        for got in gets:
            total += got[:, cols].astype(jnp.float32)
        total = total.astype(jnp.bfloat16)
        for j, send in enumerate(sends):
            send[:, cols] = total[j * tile : (j + 1) * tile]


def turns(size, order):
    return [m for m in order if m < size] + [m for m in range(1, size) if m not in order]


def cost(flops, accessed):
    return pl.CostEstimate(flops=int(flops), bytes_accessed=int(accessed), transcendentals=0)


def shards(fine_model, resample, lateral, shift, source, receiver):
    n_freq, n_slab = lax.axis_size("freq"), lax.axis_size("slab")
    n_chips = n_freq // 2
    oper, src, rec = resample[0], source[0], receiver[0]
    depth, width = src.shape
    n_fine = oper.shape[1]
    tall = depth + 2 * HALO
    where = jnp.stack([lax.axis_index("freq"), lax.axis_index("slab")]).astype(jnp.int32)
    f32, bf16 = jnp.float32, jnp.bfloat16

    line = dict((m, xor_permute(fine_model, "slab", m)) for m in turns(n_slab, Z_ORDER))
    line = [line[m] for m in range(1, n_slab)]
    edges = jnp.concatenate([src[:HALO], oper[:HALO].astype(f32)], axis=1)
    edges_last = jnp.concatenate([src[depth - HALO :], oper[depth - HALO :].astype(f32)], axis=1)
    oper_other = xor_permute(oper, "freq", 1)
    line, edges, edges_last, lateral, src, rec, oper, oper_other = lax.optimization_barrier(
        (line, edges, edges_last, lateral, src, rec, oper, oper_other)
    )
    line = jnp.concatenate([fine_model] + line, axis=0)
    plane = dict((m, xor_permute(line, "freq", 2 * m)) for m in turns(n_chips, XY_ORDER))
    plane = [line] + [plane[m] for m in range(1, n_chips)]
    odd = lax.rem(lax.axis_index("slab"), 2) == 1
    mid = [(i, i + 1) for i in range(1, n_slab - 1, 2)]
    far = lax.ppermute(jnp.where(odd, edges_last, edges), "slab", mid + [(j, i) for i, j in mid])
    near = lax.ppermute(jnp.where(odd, edges, edges_last), "slab", [(i, i ^ 1) for i in range(n_slab)])

    tile = fine_model.shape[0]
    order = [(2 * m + b, j) for m in range(n_chips) for b in range(2) for j in range(n_slab)]
    lateral, src, rec, moved, turned = stage(where, order, n_freq, n_slab, tile, oper, oper_other, lateral, src, rec)
    far, near, plane[1] = lax.optimization_barrier((far, near, plane[1]))
    above = jnp.where(odd, near, far)
    below = jnp.where(odd, far, near)
    blocks = []
    for block in plane:
        blocks += [block, xor_permute(block, "freq", 1)]

    part = pl.pallas_call(
        functools.partial(solve_kernel, len(blocks), n_slab),
        out_shape=pltpu.VMEM((depth, width), bf16),
        in_specs=[SMEM, SMEM] + [VMEM] * (len(blocks) + 9),
        out_specs=VMEM,
        scratch_shapes=[
            pltpu.VMEM((tall, width), f32),
            pltpu.VMEM((2, tall, width), f32),
            pltpu.VMEM((2, tall, width), bf16),
        ],
        compiler_params=pltpu.CompilerParams(vmem_limit_bytes=12 * MIB),
        cost_estimate=cost(2 * (SWEEPS - 1) * tall * width * width, 2 * width * width),
        name="solve",
    )(
        where, shift, *blocks, oper, above[:, width:], below[:, width:], src, above[:, :width], below[:, :width],
        rec, lateral, moved,
    )
    tile = n_fine // (n_freq * n_slab)
    keep, sends, level = back(turned, part, tile)
    gets = [xor_permute(sends[m - 1], "freq", 2 * m) for m in turns(n_chips, XYB_ORDER)]

    sends = pl.pallas_call(
        functools.partial(plane_kernel, n_chips, tile),
        out_shape=[jax.ShapeDtypeStruct((tile, width), bf16)] * (n_slab - 1),
        in_specs=[VMEM] * n_chips,
        out_specs=[VMEM] * (n_slab - 1),
        compiler_params=pltpu.CompilerParams(vmem_limit_bytes=6 * MIB),
        cost_estimate=cost(0, 4 * n_slab * tile * width * (n_chips + 1)),
        name="plane",
    )(keep, *gets)
    own = keep[:tile]
    for m in turns(n_chips, XYB2_ORDER):
        own = own + xor_permute(level[m - 1], "freq", 2 * m).astype(f32)
    for m in turns(n_slab, ZB_ORDER):
        own = own + xor_permute(sends[m - 1], "slab", m).astype(f32)
    return own


def back(turned, part, tile):
    n_chips = lax.axis_size("freq") // 2
    rows, width = turned.shape[0] // n_chips, part.shape[1]
    others = n_chips - 1
    keep, *sends = pl.pallas_call(
        functools.partial(back_kernel, n_chips, tile),
        out_shape=[jax.ShapeDtypeStruct((rows, width), jnp.float32)]
        + [jax.ShapeDtypeStruct((rows - tile, width), jnp.bfloat16)] * others
        + [jax.ShapeDtypeStruct((tile, width), jnp.bfloat16)] * others,
        in_specs=[VMEM] * 3,
        out_specs=[VMEM] * (2 * n_chips - 1),
        compiler_params=pltpu.CompilerParams(vmem_limit_bytes=6 * MIB),
        cost_estimate=cost(2 * turned.size * width, 4 * n_chips * rows * width),
        name="back",
    )(turned, part, xor_permute(part, "freq", 1))
    return keep, sends[:others], sends[others:]


def solution(mesh):
    in_specs = (
        P(("freq", "slab"), None),
        P("freq", "slab", None),
        P(),
        P("freq"),
        P("freq", "slab", None),
        P("freq", "slab", None),
    )
    out_specs = P(("freq", "slab"), None)
    return jax.shard_map(shards, mesh=mesh, in_specs=in_specs, out_specs=out_specs, check_vma=False)
```

```python
import functools

import jax
import jax.numpy as jnp
from jax import lax
from jax.experimental import pallas as pl
from jax.experimental.pallas import tpu as pltpu
from jax.sharding import PartitionSpec as P

SWEEPS = 8
HALO = 8
CUT = 2
Z_ORDER = (1, 2, 3)
XY_ORDER = (3, 2, 1)
XYB_ORDER = (3, 2, 1)
ZB_ORDER = (1, 2, 3)
XYB2_ORDER = (1, 2, 3)
TILE = 256
MIB = 1 << 20
VMEM = pl.BlockSpec(memory_space=pltpu.VMEM)
SMEM = pl.BlockSpec(memory_space=pltpu.SMEM)


def xor_permute(value, axis, mask):
    size = lax.axis_size(axis)
    return lax.ppermute(value, axis, [(i, i ^ mask) for i in range(size)])


def solve_kernel(n_blocks, n_slab, where, factor, *refs):
    blocks = refs[:n_blocks]
    oper, oper_up, oper_down, src, src_up, src_down, rec, lateral, moved = refs[n_blocks : n_blocks + 9]
    out, inverse, field, field_lo = refs[n_blocks + 9 :]
    slab = where[1]
    depth, width = src.shape
    tall = depth + 2 * HALO

    def source(cols):
        return jnp.concatenate([src_up[:, cols], src[:, cols], src_down[:, cols]], axis=0)

    rows = jnp.concatenate([oper_up[...], oper[...].astype(jnp.float32), oper_down[...]], axis=0)
    basis = jnp.dot(rows.astype(jnp.bfloat16), moved[...], preferred_element_type=jnp.float32).astype(jnp.bfloat16)
    at = lax.broadcasted_iota(jnp.int32, (tall, TILE), 0) - HALO + slab * depth
    inside = jnp.logical_and(at >= 0, at < n_slab * depth)
    for n in range(0, width, TILE):
        cols = slice(n, n + TILE)
        fine = jnp.concatenate([block[:, cols] for block in blocks], axis=0)
        coarse = jnp.dot(basis, fine, preferred_element_type=jnp.float32)
        damped = jnp.where(inside, 1.0 / (4.0 + factor[0] * coarse * coarse), 0.0)
        inverse[:, cols] = damped
        first = source(cols) * damped
        field[0, :, cols] = first
        field_lo[0, :, cols] = first.astype(jnp.bfloat16)
    for sweep in range(1, SWEEPS - 1):
        old, new = (sweep - 1) % 2, sweep % 2
        for n in range(0, width, TILE):
            cols = slice(n, n + TILE)
            side = jnp.dot(field_lo[old], lateral[:, cols], preferred_element_type=jnp.float32)
            before = field[old, :, cols]
            beside = pltpu.roll(before, 1, 0) + pltpu.roll(before, tall - 1, 0)
            after = (source(cols) + 0.5 * beside + side) * inverse[:, cols]
            field[new, :, cols] = after
            field_lo[new, :, cols] = after.astype(jnp.bfloat16)
    old = (SWEEPS - 2) % 2
    mine = slice(HALO, HALO + depth)
    for n in range(0, width, TILE):
        cols = slice(n, n + TILE)
        side = jnp.dot(field_lo[old], lateral[:, cols], preferred_element_type=jnp.float32)
        before = field[old, :, cols]
        beside = pltpu.roll(before, 1, 0) + pltpu.roll(before, tall - 1, 0)
        after = (src[:, cols] + 0.5 * beside[mine] + side[mine]) * inverse[mine, cols]
        out[:, cols] = (after * rec[:, cols]).astype(jnp.bfloat16)


def stage_kernel(order, n_freq, n_slab, tile, where, oper, oper_other, *refs):
    count = (len(refs) - 4) // 2
    moved, turned, sems, upright = refs[-4:]
    copies = [pltpu.make_async_copy(refs[i], refs[count + i], sems.at[i]) for i in range(count)]
    for copy in copies:
        copy.start()
    freq, slab = where[0], where[1]
    size = moved.shape[0]
    place = lax.broadcasted_iota(jnp.int32, (1, size), 1)
    held = jnp.zeros((1, size), jnp.int32)
    for t, (g, j) in enumerate(order):
        begin = ((freq ^ g) * n_slab + (slab ^ j)) * tile
        held = jnp.where(place >= t * tile, begin + place - t * tile, held)
    step = min(size, 128)
    for n in range(0, size, step):
        row = lax.broadcasted_iota(jnp.int32, (step, size), 0) + n
        moved[n : n + step, :] = jnp.where(row == held, 1.0, 0.0).astype(jnp.bfloat16)
    core, chip = lax.rem(freq, 2), lax.div(freq, 2)
    half = n_slab * tile
    depth = oper.shape[0]
    for m in range(n_freq // 2):
        for b, ref in enumerate((oper, oper_other)):
            at = pl.multiple_of((chip ^ m) * (2 * half), 2 * half)
            pair = ref[:, pl.ds(at, 2 * half)].astype(jnp.float32)
            mine = jnp.where(core == 0, pair[:, :half], pair[:, half:])
            upright[m, :, b * depth : (b + 1) * depth] = mine.T
    for m in range(n_freq // 2):
        for j in range(n_slab):
            at = pl.ds(pl.multiple_of((slab ^ j) * tile, tile), tile)
            begin = m * half + j * tile
            turned[begin : begin + tile, :] = upright[m, at, :].astype(jnp.bfloat16)
    for copy in copies:
        copy.wait()


def stage(where, order, n_freq, n_slab, tile, oper, oper_other, *arrays):
    size, depth = oper.shape[1], oper.shape[0]
    results = [pltpu.VMEM(a.shape, a.dtype) for a in arrays]
    results += [pltpu.VMEM((size, size), jnp.bfloat16), pltpu.VMEM((size // 2, 2 * depth), jnp.bfloat16)]
    held = sum(a.size * a.dtype.itemsize for a in arrays) + 2 * size * size + 2 * size * depth
    return pl.pallas_call(
        functools.partial(stage_kernel, order, n_freq, n_slab, tile),
        out_shape=results,
        in_specs=[SMEM, VMEM, VMEM] + [pl.BlockSpec(memory_space=pl.ANY)] * len(arrays),
        out_specs=[VMEM] * len(results),
        scratch_shapes=[
            pltpu.SemaphoreType.DMA((len(arrays),)),
            pltpu.VMEM((n_freq // 2, n_slab * tile, 2 * depth), jnp.float32),
        ],
        compiler_params=pltpu.CompilerParams(vmem_limit_bytes=58 * MIB - held),
        cost_estimate=cost(0, 2 * held),
        name="stage",
    )(where, oper, oper_other, *arrays)


def back_kernel(n_chips, tile, turned, part, part_other, keep, *sends):
    half, width = keep.shape
    far, near = sends[: n_chips - 1], sends[n_chips - 1 :]
    for n in range(0, width, TILE):
        cols = slice(n, n + TILE)
        both = jnp.concatenate([part[:, cols], part_other[:, cols]], axis=0)
        total = jnp.dot(turned[...], both, preferred_element_type=jnp.float32)
        keep[:, cols] = total[:half]
        for m in range(1, n_chips):
            rows = total[m * half : (m + 1) * half].astype(jnp.bfloat16)
            near[m - 1][:, cols] = rows[: CUT * tile]
            far[m - 1][:, cols] = rows[CUT * tile :]


def plane_kernel(n_chips, tile, begin, n_keep, keep, *refs):
    gets, outs = refs[: n_chips - 1], refs[n_chips - 1 :]
    rows = gets[0].shape[0]
    for n in range(0, keep.shape[1], TILE):
        cols = slice(n, n + TILE)
        total = keep[begin : begin + rows, cols]
        for got in gets:
            total += got[:, cols].astype(jnp.float32)
        for j, out in enumerate(outs):
            out[:, cols] = total[j * tile : (j + 1) * tile].astype(out.dtype)


def turns(size, order):
    return [m for m in order if m < size] + [m for m in range(1, size) if m not in order]


def cost(flops, accessed):
    return pl.CostEstimate(flops=int(flops), bytes_accessed=int(accessed), transcendentals=0)


def shards(fine_model, resample, lateral, shift, source, receiver):
    n_freq, n_slab = lax.axis_size("freq"), lax.axis_size("slab")
    n_chips = n_freq // 2
    oper, src, rec = resample[0], source[0], receiver[0]
    depth, width = src.shape
    n_fine = oper.shape[1]
    tall = depth + 2 * HALO
    where = jnp.stack([lax.axis_index("freq"), lax.axis_index("slab")]).astype(jnp.int32)
    f32, bf16 = jnp.float32, jnp.bfloat16

    line = dict((m, xor_permute(fine_model, "slab", m)) for m in turns(n_slab, Z_ORDER))
    line = [line[m] for m in range(1, n_slab)]
    edges = jnp.concatenate([src[:HALO], oper[:HALO].astype(f32)], axis=1)
    edges_last = jnp.concatenate([src[depth - HALO :], oper[depth - HALO :].astype(f32)], axis=1)
    oper_other = xor_permute(oper, "freq", 1)
    line, edges, edges_last, lateral, src, rec, oper, oper_other = lax.optimization_barrier(
        (line, edges, edges_last, lateral, src, rec, oper, oper_other)
    )
    line = jnp.concatenate([fine_model] + line, axis=0)
    plane = dict((m, xor_permute(line, "freq", 2 * m)) for m in turns(n_chips, XY_ORDER))
    plane = [line] + [plane[m] for m in range(1, n_chips)]
    odd = lax.rem(lax.axis_index("slab"), 2) == 1
    mid = [(i, i + 1) for i in range(1, n_slab - 1, 2)]
    far = lax.ppermute(jnp.where(odd, edges_last, edges), "slab", mid + [(j, i) for i, j in mid])
    near = lax.ppermute(jnp.where(odd, edges, edges_last), "slab", [(i, i ^ 1) for i in range(n_slab)])

    tile = fine_model.shape[0]
    order = [(2 * m + b, j) for m in range(n_chips) for b in range(2) for j in range(n_slab)]
    lateral, src, rec, moved, turned = stage(where, order, n_freq, n_slab, tile, oper, oper_other, lateral, src, rec)
    far, near, plane[1] = lax.optimization_barrier((far, near, plane[1]))
    above = jnp.where(odd, near, far)
    below = jnp.where(odd, far, near)
    blocks = []
    for block in plane:
        blocks += [block, xor_permute(block, "freq", 1)]

    part = pl.pallas_call(
        functools.partial(solve_kernel, len(blocks), n_slab),
        out_shape=pltpu.VMEM((depth, width), bf16),
        in_specs=[SMEM, SMEM] + [VMEM] * (len(blocks) + 9),
        out_specs=VMEM,
        scratch_shapes=[
            pltpu.VMEM((tall, width), f32),
            pltpu.VMEM((2, tall, width), f32),
            pltpu.VMEM((2, tall, width), bf16),
        ],
        compiler_params=pltpu.CompilerParams(vmem_limit_bytes=12 * MIB),
        cost_estimate=cost(2 * (SWEEPS - 1) * tall * width * width, 2 * width * width),
        name="solve",
    )(
        where, shift, *blocks, oper, above[:, width:], below[:, width:], src, above[:, :width], below[:, :width],
        rec, lateral, moved,
    )
    tile = n_fine // (n_freq * n_slab)
    keep, sends, level = back(turned, part, tile)
    far = [xor_permute(sends[m - 1], "freq", 2 * m) for m in turns(n_chips, XYB_ORDER)]
    far = plane_sum(keep, far, tile, CUT, 0)
    near = [xor_permute(level[m - 1], "freq", 2 * m) for m in turns(n_chips, XYB2_ORDER)]
    own, *near = plane_sum(keep, near, tile, 0, 1)
    sends = [None, *near, *far]
    for m in turns(n_slab, ZB_ORDER):
        own = own + xor_permute(sends[m], "slab", m).astype(f32)
    return own


def plane_sum(keep, gets, tile, begin, n_keep):
    width, count = keep.shape[1], gets[0].shape[0] // tile
    out_shape = [jax.ShapeDtypeStruct((tile, width), jnp.float32)] * n_keep
    out_shape += [jax.ShapeDtypeStruct((tile, width), jnp.bfloat16)] * (count - n_keep)
    return pl.pallas_call(
        functools.partial(plane_kernel, len(gets) + 1, tile, begin * tile, n_keep),
        out_shape=out_shape,
        in_specs=[VMEM] * (len(gets) + 1),
        out_specs=[VMEM] * count,
        compiler_params=pltpu.CompilerParams(vmem_limit_bytes=6 * MIB),
        cost_estimate=cost(0, 4 * count * tile * width * (len(gets) + 2)),
        name="plane",
    )(keep, *gets)


def back(turned, part, tile):
    n_chips = lax.axis_size("freq") // 2
    rows, width = turned.shape[0] // n_chips, part.shape[1]
    others = n_chips - 1
    keep, *sends = pl.pallas_call(
        functools.partial(back_kernel, n_chips, tile),
        out_shape=[jax.ShapeDtypeStruct((rows, width), jnp.float32)]
        + [jax.ShapeDtypeStruct((rows - CUT * tile, width), jnp.bfloat16)] * others
        + [jax.ShapeDtypeStruct((CUT * tile, width), jnp.bfloat16)] * others,
        in_specs=[VMEM] * 3,
        out_specs=[VMEM] * (2 * n_chips - 1),
        compiler_params=pltpu.CompilerParams(vmem_limit_bytes=6 * MIB),
        cost_estimate=cost(2 * turned.size * width, 4 * n_chips * rows * width),
        name="back",
    )(turned, part, xor_permute(part, "freq", 1))
    return keep, sends[:others], sends[others:]


def solution(mesh):
    in_specs = (
        P(("freq", "slab"), None),
        P("freq", "slab", None),
        P(),
        P("freq"),
        P("freq", "slab", None),
        P("freq", "slab", None),
    )
    out_specs = P(("freq", "slab"), None)
    return jax.shard_map(shards, mesh=mesh, in_specs=in_specs, out_specs=out_specs, check_vma=False)
```

```python
import functools

import jax
import jax.numpy as jnp
from jax import lax
from jax.experimental import pallas as pl
from jax.experimental.pallas import tpu as pltpu
from jax.sharding import PartitionSpec as P

SWEEPS = 8
HALO = 8
CUT = 2
Z_ORDER = (1, 2, 3)
XY_ORDER = (3, 2, 1)
XYB_ORDER = (3, 2, 1)
ZB_ORDER = (1, 2, 3)
XYB2_ORDER = (1, 2, 3)
TILE = 256
MIB = 1 << 20
VMEM = pl.BlockSpec(memory_space=pltpu.VMEM)
SMEM = pl.BlockSpec(memory_space=pltpu.SMEM)


def xor_permute(value, axis, mask):
    size = lax.axis_size(axis)
    return lax.ppermute(value, axis, [(i, i ^ mask) for i in range(size)])


def solve_kernel(n_blocks, n_slab, where, factor, *refs):
    blocks = refs[:n_blocks]
    oper, oper_up, oper_down, src, src_up, src_down, rec, lateral, moved = refs[n_blocks : n_blocks + 9]
    out, inverse, field, field_lo, middle = refs[n_blocks + 9 :]
    slab = where[1]
    depth, width = src.shape
    tall = depth + 2 * HALO

    def source(cols):
        return jnp.concatenate([src_up[:, cols], src[:, cols], src_down[:, cols]], axis=0)

    rows = jnp.concatenate([oper_up[...], oper[...].astype(jnp.float32), oper_down[...]], axis=0)
    basis = jnp.dot(rows.astype(jnp.bfloat16), moved[...], preferred_element_type=jnp.float32).astype(jnp.bfloat16)
    at = lax.broadcasted_iota(jnp.int32, (tall, TILE), 0) - HALO + slab * depth
    inside = jnp.logical_and(at >= 0, at < n_slab * depth)
    for n in range(0, width, TILE):
        cols = slice(n, n + TILE)
        fine = jnp.concatenate([block[:, cols] for block in blocks], axis=0)
        coarse = jnp.dot(basis, fine, preferred_element_type=jnp.float32)
        damped = jnp.where(inside, 1.0 / (4.0 + factor[0] * coarse * coarse), 0.0)
        inverse[:, cols] = damped
        first = source(cols) * damped
        field[0, :, cols] = first
        field_lo[0, :, cols] = first.astype(jnp.bfloat16)
    for sweep in range(1, SWEEPS - 1):
        old, new = (sweep - 1) % 2, sweep % 2
        for n in range(0, width, TILE):
            cols = slice(n, n + TILE)
            side = jnp.dot(field_lo[old], lateral[:, cols], preferred_element_type=jnp.float32)
            before = field[old, :, cols]
            beside = pltpu.roll(before, 1, 0) + pltpu.roll(before, tall - 1, 0)
            after = (source(cols) + 0.5 * beside + side) * inverse[:, cols]
            field[new, :, cols] = after
            if sweep < SWEEPS - 2:
                field_lo[new, :, cols] = after.astype(jnp.bfloat16)
            else:
                middle[:, cols] = after[HALO : HALO + depth].astype(jnp.bfloat16)
    old = (SWEEPS - 2) % 2
    mine = slice(HALO, HALO + depth)
    for n in range(0, width, TILE):
        cols = slice(n, n + TILE)
        side = jnp.dot(middle[...], lateral[:, cols], preferred_element_type=jnp.float32)
        before = field[old, :, cols]
        beside = pltpu.roll(before, 1, 0) + pltpu.roll(before, tall - 1, 0)
        after = (src[:, cols] + 0.5 * beside[mine] + side) * inverse[mine, cols]
        out[:, cols] = (after * rec[:, cols]).astype(jnp.bfloat16)


def stage_kernel(order, n_freq, n_slab, tile, where, oper, oper_other, *refs):
    count = (len(refs) - 4) // 2
    moved, turned, sems, upright = refs[-4:]
    copies = [pltpu.make_async_copy(refs[i], refs[count + i], sems.at[i]) for i in range(count)]
    for copy in copies:
        copy.start()
    freq, slab = where[0], where[1]
    size = moved.shape[0]
    place = lax.broadcasted_iota(jnp.int32, (1, size), 1)
    held = jnp.zeros((1, size), jnp.int32)
    for t, (g, j) in enumerate(order):
        begin = ((freq ^ g) * n_slab + (slab ^ j)) * tile
        held = jnp.where(place >= t * tile, begin + place - t * tile, held)
    step = min(size, 128)
    for n in range(0, size, step):
        row = lax.broadcasted_iota(jnp.int32, (step, size), 0) + n
        moved[n : n + step, :] = jnp.where(row == held, 1.0, 0.0).astype(jnp.bfloat16)
    core, chip = lax.rem(freq, 2), lax.div(freq, 2)
    half = n_slab * tile
    depth = oper.shape[0]
    for m in range(n_freq // 2):
        for b, ref in enumerate((oper, oper_other)):
            at = pl.multiple_of((chip ^ m) * (2 * half), 2 * half)
            pair = ref[:, pl.ds(at, 2 * half)].astype(jnp.float32)
            mine = jnp.where(core == 0, pair[:, :half], pair[:, half:])
            upright[m, :, b * depth : (b + 1) * depth] = mine.T
    for m in range(n_freq // 2):
        for j in range(n_slab):
            at = pl.ds(pl.multiple_of((slab ^ j) * tile, tile), tile)
            begin = m * half + j * tile
            turned[begin : begin + tile, :] = upright[m, at, :].astype(jnp.bfloat16)
    for copy in copies:
        copy.wait()


def stage(where, order, n_freq, n_slab, tile, oper, oper_other, *arrays):
    size, depth = oper.shape[1], oper.shape[0]
    results = [pltpu.VMEM(a.shape, a.dtype) for a in arrays]
    results += [pltpu.VMEM((size, size), jnp.bfloat16), pltpu.VMEM((size // 2, 2 * depth), jnp.bfloat16)]
    held = sum(a.size * a.dtype.itemsize for a in arrays) + 2 * size * size + 2 * size * depth
    return pl.pallas_call(
        functools.partial(stage_kernel, order, n_freq, n_slab, tile),
        out_shape=results,
        in_specs=[SMEM, VMEM, VMEM] + [pl.BlockSpec(memory_space=pl.ANY)] * len(arrays),
        out_specs=[VMEM] * len(results),
        scratch_shapes=[
            pltpu.SemaphoreType.DMA((len(arrays),)),
            pltpu.VMEM((n_freq // 2, n_slab * tile, 2 * depth), jnp.float32),
        ],
        compiler_params=pltpu.CompilerParams(vmem_limit_bytes=58 * MIB - held),
        cost_estimate=cost(0, 2 * held),
        name="stage",
    )(where, oper, oper_other, *arrays)


def back_kernel(n_chips, tile, turned, part, part_other, keep, *sends):
    half, width = keep.shape
    far, near = sends[: n_chips - 1], sends[n_chips - 1 :]
    for n in range(0, width, TILE):
        cols = slice(n, n + TILE)
        both = jnp.concatenate([part[:, cols], part_other[:, cols]], axis=0)
        total = jnp.dot(turned[...], both, preferred_element_type=jnp.float32)
        keep[:, cols] = total[:half]
        for m in range(1, n_chips):
            rows = total[m * half : (m + 1) * half].astype(jnp.bfloat16)
            near[m - 1][:, cols] = rows[: CUT * tile]
            far[m - 1][:, cols] = rows[CUT * tile :]


def plane_kernel(n_chips, tile, begin, keep, *refs):
    gets, outs = refs[: n_chips - 1], refs[n_chips - 1 :]
    rows = gets[0].shape[0]
    for n in range(0, keep.shape[1], TILE):
        cols = slice(n, n + TILE)
        total = keep[begin : begin + rows, cols]
        for got in gets:
            total += got[:, cols].astype(jnp.float32)
        for j, out in enumerate(outs):
            out[:, cols] = total[j * tile : (j + 1) * tile].astype(out.dtype)


def turns(size, order):
    return [m for m in order if m < size] + [m for m in range(1, size) if m not in order]


def cost(flops, accessed):
    return pl.CostEstimate(flops=int(flops), bytes_accessed=int(accessed), transcendentals=0)


def shards(fine_model, resample, lateral, shift, source, receiver):
    n_freq, n_slab = lax.axis_size("freq"), lax.axis_size("slab")
    n_chips = n_freq // 2
    oper, src, rec = resample[0], source[0], receiver[0]
    depth, width = src.shape
    n_fine = oper.shape[1]
    tall = depth + 2 * HALO
    where = jnp.stack([lax.axis_index("freq"), lax.axis_index("slab")]).astype(jnp.int32)
    f32, bf16 = jnp.float32, jnp.bfloat16

    line = dict((m, xor_permute(fine_model, "slab", m)) for m in turns(n_slab, Z_ORDER))
    line = [line[m] for m in range(1, n_slab)]
    edges = jnp.concatenate([src[:HALO], oper[:HALO].astype(f32)], axis=1)
    edges_last = jnp.concatenate([src[depth - HALO :], oper[depth - HALO :].astype(f32)], axis=1)
    oper_other = xor_permute(oper, "freq", 1)
    line, edges, edges_last, lateral, src, rec, oper, oper_other = lax.optimization_barrier(
        (line, edges, edges_last, lateral, src, rec, oper, oper_other)
    )
    line = jnp.concatenate([fine_model] + line, axis=0)
    plane = dict((m, xor_permute(line, "freq", 2 * m)) for m in turns(n_chips, XY_ORDER))
    plane = [line] + [plane[m] for m in range(1, n_chips)]
    odd = lax.rem(lax.axis_index("slab"), 2) == 1
    mid = [(i, i + 1) for i in range(1, n_slab - 1, 2)]
    far = lax.ppermute(jnp.where(odd, edges_last, edges), "slab", mid + [(j, i) for i, j in mid])
    near = lax.ppermute(jnp.where(odd, edges, edges_last), "slab", [(i, i ^ 1) for i in range(n_slab)])

    tile = fine_model.shape[0]
    order = [(2 * m + b, j) for m in range(n_chips) for b in range(2) for j in range(n_slab)]
    lateral, src, rec, moved, turned = stage(where, order, n_freq, n_slab, tile, oper, oper_other, lateral, src, rec)
    near, far, plane[1] = lax.optimization_barrier((near, far, plane[1]))
    above = jnp.where(odd, near, far)
    below = jnp.where(odd, far, near)
    blocks = []
    for block in plane:
        blocks += [block, xor_permute(block, "freq", 1)]

    part = pl.pallas_call(
        functools.partial(solve_kernel, len(blocks), n_slab),
        out_shape=pltpu.VMEM((depth, width), bf16),
        in_specs=[SMEM, SMEM] + [VMEM] * (len(blocks) + 9),
        out_specs=VMEM,
        scratch_shapes=[
            pltpu.VMEM((tall, width), f32),
            pltpu.VMEM((2, tall, width), f32),
            pltpu.VMEM((2, tall, width), bf16),
            pltpu.VMEM((depth, width), bf16),
        ],
        compiler_params=pltpu.CompilerParams(vmem_limit_bytes=12 * MIB),
        cost_estimate=cost(2 * (SWEEPS - 1) * tall * width * width, 2 * width * width),
        name="solve",
    )(
        where, shift, *blocks, oper, above[:, width:], below[:, width:], src, above[:, :width], below[:, :width],
        rec, lateral, moved,
    )
    tile = n_fine // (n_freq * n_slab)
    keep, sends, level = back(turned, part, tile)
    far = [xor_permute(sends[m - 1], "freq", 2 * m) for m in turns(n_chips, XYB_ORDER)]
    far = plane_sum(keep, far, tile, CUT, 0)
    near = [xor_permute(level[m - 1], "freq", 2 * m) for m in turns(n_chips, XYB2_ORDER)]
    own, *near = plane_sum(keep, near, tile, 0, 1)
    sends = [None, *near, *far]
    for m in turns(n_slab, ZB_ORDER):
        own = own + xor_permute(sends[m], "slab", m).astype(f32)
    return own


def plane_sum(keep, gets, tile, begin, n_keep):
    width, count = keep.shape[1], gets[0].shape[0] // tile
    out_shape = [jax.ShapeDtypeStruct((tile, width), jnp.float32)] * n_keep
    out_shape += [jax.ShapeDtypeStruct((tile, width), jnp.bfloat16)] * (count - n_keep)
    return pl.pallas_call(
        functools.partial(plane_kernel, len(gets) + 1, tile, begin * tile),
        out_shape=out_shape,
        in_specs=[VMEM] * (len(gets) + 1),
        out_specs=[VMEM] * count,
        compiler_params=pltpu.CompilerParams(vmem_limit_bytes=6 * MIB),
        cost_estimate=cost(0, 4 * count * tile * width * (len(gets) + 2)),
        name="plane",
    )(keep, *gets)


def back(turned, part, tile):
    n_chips = lax.axis_size("freq") // 2
    rows, width = turned.shape[0] // n_chips, part.shape[1]
    others = n_chips - 1
    keep, *sends = pl.pallas_call(
        functools.partial(back_kernel, n_chips, tile),
        out_shape=[jax.ShapeDtypeStruct((rows, width), jnp.float32)]
        + [jax.ShapeDtypeStruct((rows - CUT * tile, width), jnp.bfloat16)] * others
        + [jax.ShapeDtypeStruct((CUT * tile, width), jnp.bfloat16)] * others,
        in_specs=[VMEM] * 3,
        out_specs=[VMEM] * (2 * n_chips - 1),
        compiler_params=pltpu.CompilerParams(vmem_limit_bytes=6 * MIB),
        cost_estimate=cost(2 * turned.size * width, 4 * n_chips * rows * width),
        name="back",
    )(turned, part, xor_permute(part, "freq", 1))
    return keep, sends[:others], sends[others:]


def solution(mesh):
    in_specs = (
        P(("freq", "slab"), None),
        P("freq", "slab", None),
        P(),
        P("freq"),
        P("freq", "slab", None),
        P("freq", "slab", None),
    )
    out_specs = P(("freq", "slab"), None)
    return jax.shard_map(shards, mesh=mesh, in_specs=in_specs, out_specs=out_specs, check_vma=False)
```

```python
import functools

import jax
import jax.numpy as jnp
from jax import lax
from jax.experimental import pallas as pl
from jax.experimental.pallas import tpu as pltpu
from jax.sharding import PartitionSpec as P

SWEEPS = 8
HALO = 8
CUT = 2
Z_ORDER = (1, 2, 3)
XY_ORDER = (3, 2, 1)
XYB_ORDER = (3, 2, 1)
ZB_ORDER = (1, 3, 2)
XYB2_ORDER = (1, 2, 3)
TILE = 256
MIB = 1 << 20
VMEM = pl.BlockSpec(memory_space=pltpu.VMEM)
SMEM = pl.BlockSpec(memory_space=pltpu.SMEM)


def xor_permute(value, axis, mask):
    size = lax.axis_size(axis)
    return lax.ppermute(value, axis, [(i, i ^ mask) for i in range(size)])


def solve_kernel(n_blocks, n_slab, where, factor, *refs):
    blocks = refs[:n_blocks]
    oper, oper_up, oper_down, src, src_up, src_down, rec, lateral, moved = refs[n_blocks : n_blocks + 9]
    out, inverse, field, field_lo, middle = refs[n_blocks + 9 :]
    slab = where[1]
    depth, width = src.shape
    tall = depth + 2 * HALO

    def source(cols):
        return jnp.concatenate([src_up[:, cols], src[:, cols], src_down[:, cols]], axis=0)

    rows = jnp.concatenate([oper_up[...], oper[...].astype(jnp.float32), oper_down[...]], axis=0)
    basis = jnp.dot(rows.astype(jnp.bfloat16), moved[...], preferred_element_type=jnp.float32).astype(jnp.bfloat16)
    at = lax.broadcasted_iota(jnp.int32, (tall, TILE), 0) - HALO + slab * depth
    inside = jnp.logical_and(at >= 0, at < n_slab * depth)
    for n in range(0, width, TILE):
        cols = slice(n, n + TILE)
        fine = jnp.concatenate([block[:, cols] for block in blocks], axis=0)
        coarse = jnp.dot(basis, fine, preferred_element_type=jnp.float32)
        damped = jnp.where(inside, 1.0 / (4.0 + factor[0] * coarse * coarse), 0.0)
        inverse[:, cols] = damped
        first = source(cols) * damped
        field[0, :, cols] = first
        field_lo[0, :, cols] = first.astype(jnp.bfloat16)
    for sweep in range(1, SWEEPS - 1):
        old, new = (sweep - 1) % 2, sweep % 2
        for n in range(0, width, TILE):
            cols = slice(n, n + TILE)
            side = jnp.dot(field_lo[old], lateral[:, cols], preferred_element_type=jnp.float32)
            before = field[old, :, cols]
            beside = pltpu.roll(before, 1, 0) + pltpu.roll(before, tall - 1, 0)
            after = (source(cols) + 0.5 * beside + side) * inverse[:, cols]
            field[new, :, cols] = after
            if sweep < SWEEPS - 2:
                field_lo[new, :, cols] = after.astype(jnp.bfloat16)
            else:
                middle[:, cols] = after[HALO : HALO + depth].astype(jnp.bfloat16)
    old = (SWEEPS - 2) % 2
    mine = slice(HALO, HALO + depth)
    for n in range(0, width, TILE):
        cols = slice(n, n + TILE)
        side = jnp.dot(middle[...], lateral[:, cols], preferred_element_type=jnp.float32)
        before = field[old, :, cols]
        beside = pltpu.roll(before, 1, 0) + pltpu.roll(before, tall - 1, 0)
        after = (src[:, cols] + 0.5 * beside[mine] + side) * inverse[mine, cols]
        out[:, cols] = (after * rec[:, cols]).astype(jnp.bfloat16)


def stage_kernel(order, n_freq, n_slab, tile, where, oper, oper_other, *refs):
    count = (len(refs) - 4) // 2
    moved, turned, sems, upright = refs[-4:]
    copies = [pltpu.make_async_copy(refs[i], refs[count + i], sems.at[i]) for i in range(count)]
    for copy in copies:
        copy.start()
    freq, slab = where[0], where[1]
    size = moved.shape[0]
    place = lax.broadcasted_iota(jnp.int32, (1, size), 1)
    held = jnp.zeros((1, size), jnp.int32)
    for t, (g, j) in enumerate(order):
        begin = ((freq ^ g) * n_slab + (slab ^ j)) * tile
        held = jnp.where(place >= t * tile, begin + place - t * tile, held)
    step = min(size, 128)
    for n in range(0, size, step):
        row = lax.broadcasted_iota(jnp.int32, (step, size), 0) + n
        moved[n : n + step, :] = jnp.where(row == held, 1.0, 0.0).astype(jnp.bfloat16)
    core, chip = lax.rem(freq, 2), lax.div(freq, 2)
    half = n_slab * tile
    depth = oper.shape[0]
    for m in range(n_freq // 2):
        for b, ref in enumerate((oper, oper_other)):
            at = pl.multiple_of((chip ^ m) * (2 * half), 2 * half)
            pair = ref[:, pl.ds(at, 2 * half)].astype(jnp.float32)
            mine = jnp.where(core == 0, pair[:, :half], pair[:, half:])
            upright[m, :, b * depth : (b + 1) * depth] = mine.T
    for m in range(n_freq // 2):
        for j in range(n_slab):
            at = pl.ds(pl.multiple_of((slab ^ j) * tile, tile), tile)
            begin = m * half + j * tile
            turned[begin : begin + tile, :] = upright[m, at, :].astype(jnp.bfloat16)
    for copy in copies:
        copy.wait()


def stage(where, order, n_freq, n_slab, tile, oper, oper_other, *arrays):
    size, depth = oper.shape[1], oper.shape[0]
    results = [pltpu.VMEM(a.shape, a.dtype) for a in arrays]
    results += [pltpu.VMEM((size, size), jnp.bfloat16), pltpu.VMEM((size // 2, 2 * depth), jnp.bfloat16)]
    held = sum(a.size * a.dtype.itemsize for a in arrays) + 2 * size * size + 2 * size * depth
    return pl.pallas_call(
        functools.partial(stage_kernel, order, n_freq, n_slab, tile),
        out_shape=results,
        in_specs=[SMEM, VMEM, VMEM] + [pl.BlockSpec(memory_space=pl.ANY)] * len(arrays),
        out_specs=[VMEM] * len(results),
        scratch_shapes=[
            pltpu.SemaphoreType.DMA((len(arrays),)),
            pltpu.VMEM((n_freq // 2, n_slab * tile, 2 * depth), jnp.float32),
        ],
        compiler_params=pltpu.CompilerParams(vmem_limit_bytes=58 * MIB - held),
        cost_estimate=cost(0, 2 * held),
        name="stage",
    )(where, oper, oper_other, *arrays)


def back_kernel(n_chips, tile, turned, part, part_other, keep, *sends):
    half, width = keep.shape
    far, near = sends[: n_chips - 1], sends[n_chips - 1 :]
    for n in range(0, width, TILE):
        cols = slice(n, n + TILE)
        both = jnp.concatenate([part[:, cols], part_other[:, cols]], axis=0)
        total = jnp.dot(turned[...], both, preferred_element_type=jnp.float32)
        keep[:, cols] = total[:half]
        for m in range(1, n_chips):
            rows = total[m * half : (m + 1) * half].astype(jnp.bfloat16)
            near[m - 1][:, cols] = rows[: CUT * tile]
            far[m - 1][:, cols] = rows[CUT * tile :]


def plane_kernel(n_chips, tile, begin, keep, *refs):
    gets, outs = refs[: n_chips - 1], refs[n_chips - 1 :]
    rows = gets[0].shape[0]
    for n in range(0, keep.shape[1], TILE):
        cols = slice(n, n + TILE)
        total = keep[begin : begin + rows, cols]
        for got in gets:
            total += got[:, cols].astype(jnp.float32)
        for j, out in enumerate(outs):
            out[:, cols] = total[j * tile : (j + 1) * tile].astype(out.dtype)


def turns(size, order):
    return [m for m in order if m < size] + [m for m in range(1, size) if m not in order]


def cost(flops, accessed):
    return pl.CostEstimate(flops=int(flops), bytes_accessed=int(accessed), transcendentals=0)


def shards(fine_model, resample, lateral, shift, source, receiver):
    n_freq, n_slab = lax.axis_size("freq"), lax.axis_size("slab")
    n_chips = n_freq // 2
    oper, src, rec = resample[0], source[0], receiver[0]
    depth, width = src.shape
    n_fine = oper.shape[1]
    tall = depth + 2 * HALO
    where = jnp.stack([lax.axis_index("freq"), lax.axis_index("slab")]).astype(jnp.int32)
    f32, bf16 = jnp.float32, jnp.bfloat16

    line = dict((m, xor_permute(fine_model, "slab", m)) for m in turns(n_slab, Z_ORDER))
    line = [line[m] for m in range(1, n_slab)]
    edges = jnp.concatenate([src[:HALO], oper[:HALO].astype(f32)], axis=1)
    edges_last = jnp.concatenate([src[depth - HALO :], oper[depth - HALO :].astype(f32)], axis=1)
    oper_other = xor_permute(oper, "freq", 1)
    line, edges, edges_last, lateral, src, rec, oper, oper_other = lax.optimization_barrier(
        (line, edges, edges_last, lateral, src, rec, oper, oper_other)
    )
    line = jnp.concatenate([fine_model] + line, axis=0)
    plane = dict((m, xor_permute(line, "freq", 2 * m)) for m in turns(n_chips, XY_ORDER))
    plane = [line] + [plane[m] for m in range(1, n_chips)]
    odd = lax.rem(lax.axis_index("slab"), 2) == 1
    mid = [(i, i + 1) for i in range(1, n_slab - 1, 2)]
    far = lax.ppermute(jnp.where(odd, edges_last, edges), "slab", mid + [(j, i) for i, j in mid])
    near = lax.ppermute(jnp.where(odd, edges, edges_last), "slab", [(i, i ^ 1) for i in range(n_slab)])

    tile = fine_model.shape[0]
    order = [(2 * m + b, j) for m in range(n_chips) for b in range(2) for j in range(n_slab)]
    lateral, src, rec, moved, turned = stage(where, order, n_freq, n_slab, tile, oper, oper_other, lateral, src, rec)
    near, far, plane[1] = lax.optimization_barrier((near, far, plane[1]))
    above = jnp.where(odd, near, far)
    below = jnp.where(odd, far, near)
    blocks = []
    for block in plane:
        blocks += [block, xor_permute(block, "freq", 1)]

    part = pl.pallas_call(
        functools.partial(solve_kernel, len(blocks), n_slab),
        out_shape=pltpu.VMEM((depth, width), bf16),
        in_specs=[SMEM, SMEM] + [VMEM] * (len(blocks) + 9),
        out_specs=VMEM,
        scratch_shapes=[
            pltpu.VMEM((tall, width), f32),
            pltpu.VMEM((2, tall, width), f32),
            pltpu.VMEM((2, tall, width), bf16),
            pltpu.VMEM((depth, width), bf16),
        ],
        compiler_params=pltpu.CompilerParams(vmem_limit_bytes=12 * MIB),
        cost_estimate=cost(2 * (SWEEPS - 1) * tall * width * width, 2 * width * width),
        name="solve",
    )(
        where, shift, *blocks, oper, above[:, width:], below[:, width:], src, above[:, :width], below[:, :width],
        rec, lateral, moved,
    )
    tile = n_fine // (n_freq * n_slab)
    keep, sends, level = back(turned, part, tile)
    far = [xor_permute(sends[m - 1], "freq", 2 * m) for m in turns(n_chips, XYB_ORDER)]
    far = plane_sum(keep, far, tile, CUT, 0)
    near = [xor_permute(level[m - 1], "freq", 2 * m) for m in turns(n_chips, XYB2_ORDER)]
    own, *near = plane_sum(keep, near, tile, 0, 1)
    sends = [None, *near, *far]
    for m in turns(n_slab, ZB_ORDER):
        own = own + xor_permute(sends[m], "slab", m).astype(f32)
    return own


def plane_sum(keep, gets, tile, begin, n_keep):
    width, count = keep.shape[1], gets[0].shape[0] // tile
    out_shape = [jax.ShapeDtypeStruct((tile, width), jnp.float32)] * n_keep
    out_shape += [jax.ShapeDtypeStruct((tile, width), jnp.bfloat16)] * (count - n_keep)
    return pl.pallas_call(
        functools.partial(plane_kernel, len(gets) + 1, tile, begin * tile),
        out_shape=out_shape,
        in_specs=[VMEM] * (len(gets) + 1),
        out_specs=[VMEM] * count,
        compiler_params=pltpu.CompilerParams(vmem_limit_bytes=6 * MIB),
        cost_estimate=cost(0, 4 * count * tile * width * (len(gets) + 2)),
        name="plane",
    )(keep, *gets)


def back(turned, part, tile):
    n_chips = lax.axis_size("freq") // 2
    rows, width = turned.shape[0] // n_chips, part.shape[1]
    others = n_chips - 1
    keep, *sends = pl.pallas_call(
        functools.partial(back_kernel, n_chips, tile),
        out_shape=[jax.ShapeDtypeStruct((rows, width), jnp.float32)]
        + [jax.ShapeDtypeStruct((rows - CUT * tile, width), jnp.bfloat16)] * others
        + [jax.ShapeDtypeStruct((CUT * tile, width), jnp.bfloat16)] * others,
        in_specs=[VMEM] * 3,
        out_specs=[VMEM] * (2 * n_chips - 1),
        compiler_params=pltpu.CompilerParams(vmem_limit_bytes=6 * MIB),
        cost_estimate=cost(2 * turned.size * width, 4 * n_chips * rows * width),
        name="back",
    )(turned, part, xor_permute(part, "freq", 1))
    return keep, sends[:others], sends[others:]


def solution(mesh):
    in_specs = (
        P(("freq", "slab"), None),
        P("freq", "slab", None),
        P(),
        P("freq"),
        P("freq", "slab", None),
        P("freq", "slab", None),
    )
    out_specs = P(("freq", "slab"), None)
    return jax.shard_map(shards, mesh=mesh, in_specs=in_specs, out_specs=out_specs, check_vma=False)
```

```python
import functools

import jax
import jax.numpy as jnp
from jax import lax
from jax.experimental import pallas as pl
from jax.experimental.pallas import tpu as pltpu
from jax.sharding import PartitionSpec as P

SWEEPS = 8
HALO = 8
CUT = 2
Z_ORDER = (1, 2, 3)
XY_ORDER = (3, 2, 1)
XYB_ORDER = (3, 2, 1)
ZB_ORDER = (1, 3, 2)
XYB2_ORDER = (1, 2, 3)
TILE = 256
MIB = 1 << 20
VMEM = pl.BlockSpec(memory_space=pltpu.VMEM)
SMEM = pl.BlockSpec(memory_space=pltpu.SMEM)


def xor_permute(value, axis, mask):
    size = lax.axis_size(axis)
    return lax.ppermute(value, axis, [(i, i ^ mask) for i in range(size)])


def solve_kernel(n_blocks, n_slab, where, factor, *refs):
    blocks = refs[:n_blocks]
    oper, oper_up, oper_down, src, src_up, src_down, rec, lateral, moved = refs[n_blocks : n_blocks + 9]
    out, inverse, field, field_lo, middle = refs[n_blocks + 9 :]
    slab = where[1]
    depth, width = src.shape
    tall = depth + 2 * HALO

    def source(cols):
        return jnp.concatenate([src_up[:, cols], src[:, cols], src_down[:, cols]], axis=0)

    outer = jnp.concatenate([oper_up[...], oper_down[...]], axis=0).astype(jnp.bfloat16)
    outer = jnp.dot(outer, moved[...], preferred_element_type=jnp.float32)
    basis = jnp.concatenate([outer[:HALO], oper[...].astype(jnp.float32), outer[HALO:]], axis=0).astype(jnp.bfloat16)
    at = lax.broadcasted_iota(jnp.int32, (tall, TILE), 0) - HALO + slab * depth
    inside = jnp.logical_and(at >= 0, at < n_slab * depth)
    for n in range(0, width, TILE):
        cols = slice(n, n + TILE)
        fine = jnp.concatenate([block[:, cols] for block in blocks], axis=0)
        coarse = jnp.dot(basis, fine, preferred_element_type=jnp.float32)
        damped = jnp.where(inside, 1.0 / (4.0 + factor[0] * coarse * coarse), 0.0)
        inverse[:, cols] = damped
        first = source(cols) * damped
        field[0, :, cols] = first
        field_lo[0, :, cols] = first.astype(jnp.bfloat16)
    for sweep in range(1, SWEEPS - 1):
        old, new = (sweep - 1) % 2, sweep % 2
        for n in range(0, width, TILE):
            cols = slice(n, n + TILE)
            side = jnp.dot(field_lo[old], lateral[:, cols], preferred_element_type=jnp.float32)
            before = field[old, :, cols]
            beside = pltpu.roll(before, 1, 0) + pltpu.roll(before, tall - 1, 0)
            after = (source(cols) + 0.5 * beside + side) * inverse[:, cols]
            field[new, :, cols] = after
            if sweep < SWEEPS - 2:
                field_lo[new, :, cols] = after.astype(jnp.bfloat16)
            else:
                middle[:, cols] = after[HALO : HALO + depth].astype(jnp.bfloat16)
    old = (SWEEPS - 2) % 2
    mine = slice(HALO, HALO + depth)
    for n in range(0, width, TILE):
        cols = slice(n, n + TILE)
        side = jnp.dot(middle[...], lateral[:, cols], preferred_element_type=jnp.float32)
        before = field[old, :, cols]
        beside = pltpu.roll(before, 1, 0) + pltpu.roll(before, tall - 1, 0)
        after = (src[:, cols] + 0.5 * beside[mine] + side) * inverse[mine, cols]
        out[:, cols] = (after * rec[:, cols]).astype(jnp.bfloat16)


def stage_kernel(order, n_freq, n_slab, tile, where, oper, oper_other, *refs):
    count = (len(refs) - 5) // 2
    moved, turned, basis, sems, upright = refs[-5:]
    copies = [pltpu.make_async_copy(refs[i], refs[count + i], sems.at[i]) for i in range(count)]
    for copy in copies:
        copy.start()
    freq, slab = where[0], where[1]
    size = moved.shape[0]
    place = lax.broadcasted_iota(jnp.int32, (1, size), 1)
    held = jnp.zeros((1, size), jnp.int32)
    for t, (g, j) in enumerate(order):
        begin = ((freq ^ g) * n_slab + (slab ^ j)) * tile
        held = jnp.where(place >= t * tile, begin + place - t * tile, held)
    step = min(size, 128)
    for n in range(0, size, step):
        row = lax.broadcasted_iota(jnp.int32, (step, size), 0) + n
        moved[n : n + step, :] = jnp.where(row == held, 1.0, 0.0).astype(jnp.bfloat16)
    basis[...] = jnp.dot(oper[...], moved[...], preferred_element_type=jnp.float32).astype(jnp.bfloat16)
    core, chip = lax.rem(freq, 2), lax.div(freq, 2)
    half = n_slab * tile
    depth = oper.shape[0]
    for m in range(n_freq // 2):
        for b, ref in enumerate((oper, oper_other)):
            at = pl.multiple_of((chip ^ m) * (2 * half), 2 * half)
            pair = ref[:, pl.ds(at, 2 * half)].astype(jnp.float32)
            mine = jnp.where(core == 0, pair[:, :half], pair[:, half:])
            upright[m, :, b * depth : (b + 1) * depth] = mine.T
    for m in range(n_freq // 2):
        for j in range(n_slab):
            at = pl.ds(pl.multiple_of((slab ^ j) * tile, tile), tile)
            begin = m * half + j * tile
            turned[begin : begin + tile, :] = upright[m, at, :].astype(jnp.bfloat16)
    for copy in copies:
        copy.wait()


def stage(where, order, n_freq, n_slab, tile, oper, oper_other, *arrays):
    size, depth = oper.shape[1], oper.shape[0]
    results = [pltpu.VMEM(a.shape, a.dtype) for a in arrays]
    results += [pltpu.VMEM((size, size), jnp.bfloat16), pltpu.VMEM((size // 2, 2 * depth), jnp.bfloat16), pltpu.VMEM((depth, size), jnp.bfloat16)]
    held = sum(a.size * a.dtype.itemsize for a in arrays) + 2 * size * size + 2 * size * depth
    return pl.pallas_call(
        functools.partial(stage_kernel, order, n_freq, n_slab, tile),
        out_shape=results,
        in_specs=[SMEM, VMEM, VMEM] + [pl.BlockSpec(memory_space=pl.ANY)] * len(arrays),
        out_specs=[VMEM] * len(results),
        scratch_shapes=[
            pltpu.SemaphoreType.DMA((len(arrays),)),
            pltpu.VMEM((n_freq // 2, n_slab * tile, 2 * depth), jnp.float32),
        ],
        compiler_params=pltpu.CompilerParams(vmem_limit_bytes=58 * MIB - held),
        cost_estimate=cost(0, 2 * held),
        name="stage",
    )(where, oper, oper_other, *arrays)


def back_kernel(n_chips, tile, turned, part, part_other, keep, *sends):
    half, width = keep.shape
    far, near = sends[: n_chips - 1], sends[n_chips - 1 :]
    for n in range(0, width, TILE):
        cols = slice(n, n + TILE)
        both = jnp.concatenate([part[:, cols], part_other[:, cols]], axis=0)
        total = jnp.dot(turned[...], both, preferred_element_type=jnp.float32)
        keep[:, cols] = total[:half]
        for m in range(1, n_chips):
            rows = total[m * half : (m + 1) * half].astype(jnp.bfloat16)
            near[m - 1][:, cols] = rows[: CUT * tile]
            far[m - 1][:, cols] = rows[CUT * tile :]


def plane_kernel(n_chips, tile, begin, keep, *refs):
    gets, outs = refs[: n_chips - 1], refs[n_chips - 1 :]
    rows = gets[0].shape[0]
    for n in range(0, keep.shape[1], TILE):
        cols = slice(n, n + TILE)
        total = keep[begin : begin + rows, cols]
        for got in gets:
            total += got[:, cols].astype(jnp.float32)
        for j, out in enumerate(outs):
            out[:, cols] = total[j * tile : (j + 1) * tile].astype(out.dtype)


def turns(size, order):
    return [m for m in order if m < size] + [m for m in range(1, size) if m not in order]


def cost(flops, accessed):
    return pl.CostEstimate(flops=int(flops), bytes_accessed=int(accessed), transcendentals=0)


def shards(fine_model, resample, lateral, shift, source, receiver):
    n_freq, n_slab = lax.axis_size("freq"), lax.axis_size("slab")
    n_chips = n_freq // 2
    oper, src, rec = resample[0], source[0], receiver[0]
    depth, width = src.shape
    n_fine = oper.shape[1]
    tall = depth + 2 * HALO
    where = jnp.stack([lax.axis_index("freq"), lax.axis_index("slab")]).astype(jnp.int32)
    f32, bf16 = jnp.float32, jnp.bfloat16

    line = dict((m, xor_permute(fine_model, "slab", m)) for m in turns(n_slab, Z_ORDER))
    line = [line[m] for m in range(1, n_slab)]
    edges = jnp.concatenate([src[:HALO], oper[:HALO].astype(f32)], axis=1)
    edges_last = jnp.concatenate([src[depth - HALO :], oper[depth - HALO :].astype(f32)], axis=1)
    oper_other = xor_permute(oper, "freq", 1)
    line, edges, edges_last, lateral, src, rec, oper, oper_other = lax.optimization_barrier(
        (line, edges, edges_last, lateral, src, rec, oper, oper_other)
    )
    line = jnp.concatenate([fine_model] + line, axis=0)
    plane = dict((m, xor_permute(line, "freq", 2 * m)) for m in turns(n_chips, XY_ORDER))
    plane = [line] + [plane[m] for m in range(1, n_chips)]
    odd = lax.rem(lax.axis_index("slab"), 2) == 1
    mid = [(i, i + 1) for i in range(1, n_slab - 1, 2)]
    far = lax.ppermute(jnp.where(odd, edges_last, edges), "slab", mid + [(j, i) for i, j in mid])
    near = lax.ppermute(jnp.where(odd, edges, edges_last), "slab", [(i, i ^ 1) for i in range(n_slab)])

    tile = fine_model.shape[0]
    order = [(2 * m + b, j) for m in range(n_chips) for b in range(2) for j in range(n_slab)]
    lateral, src, rec, moved, turned, basis = stage(where, order, n_freq, n_slab, tile, oper, oper_other, lateral, src, rec)
    near, far, plane[1] = lax.optimization_barrier((near, far, plane[1]))
    above = jnp.where(odd, near, far)
    below = jnp.where(odd, far, near)
    blocks = []
    for block in plane:
        blocks += [block, xor_permute(block, "freq", 1)]

    part = pl.pallas_call(
        functools.partial(solve_kernel, len(blocks), n_slab),
        out_shape=pltpu.VMEM((depth, width), bf16),
        in_specs=[SMEM, SMEM] + [VMEM] * (len(blocks) + 9),
        out_specs=VMEM,
        scratch_shapes=[
            pltpu.VMEM((tall, width), f32),
            pltpu.VMEM((2, tall, width), f32),
            pltpu.VMEM((2, tall, width), bf16),
            pltpu.VMEM((depth, width), bf16),
        ],
        compiler_params=pltpu.CompilerParams(vmem_limit_bytes=12 * MIB),
        cost_estimate=cost(2 * (SWEEPS - 1) * tall * width * width, 2 * width * width),
        name="solve",
    )(
        where, shift, *blocks, basis, above[:, width:], below[:, width:], src, above[:, :width], below[:, :width],
        rec, lateral, moved,
    )
    tile = n_fine // (n_freq * n_slab)
    keep, sends, level = back(turned, part, tile)
    far = [xor_permute(sends[m - 1], "freq", 2 * m) for m in turns(n_chips, XYB_ORDER)]
    far = plane_sum(keep, far, tile, CUT, 0)
    near = [xor_permute(level[m - 1], "freq", 2 * m) for m in turns(n_chips, XYB2_ORDER)]
    own, *near = plane_sum(keep, near, tile, 0, 1)
    sends = [None, *near, *far]
    for m in turns(n_slab, ZB_ORDER):
        own = own + xor_permute(sends[m], "slab", m).astype(f32)
    return own


def plane_sum(keep, gets, tile, begin, n_keep):
    width, count = keep.shape[1], gets[0].shape[0] // tile
    out_shape = [jax.ShapeDtypeStruct((tile, width), jnp.float32)] * n_keep
    out_shape += [jax.ShapeDtypeStruct((tile, width), jnp.bfloat16)] * (count - n_keep)
    return pl.pallas_call(
        functools.partial(plane_kernel, len(gets) + 1, tile, begin * tile),
        out_shape=out_shape,
        in_specs=[VMEM] * (len(gets) + 1),
        out_specs=[VMEM] * count,
        compiler_params=pltpu.CompilerParams(vmem_limit_bytes=6 * MIB),
        cost_estimate=cost(0, 4 * count * tile * width * (len(gets) + 2)),
        name="plane",
    )(keep, *gets)


def back(turned, part, tile):
    n_chips = lax.axis_size("freq") // 2
    rows, width = turned.shape[0] // n_chips, part.shape[1]
    others = n_chips - 1
    keep, *sends = pl.pallas_call(
        functools.partial(back_kernel, n_chips, tile),
        out_shape=[jax.ShapeDtypeStruct((rows, width), jnp.float32)]
        + [jax.ShapeDtypeStruct((rows - CUT * tile, width), jnp.bfloat16)] * others
        + [jax.ShapeDtypeStruct((CUT * tile, width), jnp.bfloat16)] * others,
        in_specs=[VMEM] * 3,
        out_specs=[VMEM] * (2 * n_chips - 1),
        compiler_params=pltpu.CompilerParams(vmem_limit_bytes=6 * MIB),
        cost_estimate=cost(2 * turned.size * width, 4 * n_chips * rows * width),
        name="back",
    )(turned, part, xor_permute(part, "freq", 1))
    return keep, sends[:others], sends[others:]


def solution(mesh):
    in_specs = (
        P(("freq", "slab"), None),
        P("freq", "slab", None),
        P(),
        P("freq"),
        P("freq", "slab", None),
        P("freq", "slab", None),
    )
    out_specs = P(("freq", "slab"), None)
    return jax.shard_map(shards, mesh=mesh, in_specs=in_specs, out_specs=out_specs, check_vma=False)
```
